32 devices in a mesh: groups: 2 (over y), ctx: 4 (over z), head: 4 (over x, core).
Axes of the slice: x: 2, y: 2, z: 4, core: 2. Of those that a mesh axis runs over, the one named last changes fastest.
Arguments:
- queries: bfloat16 [8192, 3584], P(('groups', 'ctx'), 'head'), parts along dimension 0, may hold values from -13 to 13
- key_states: bfloat16 [8192, 512], P(('groups', 'ctx'), 'head'), parts along dimension 0, may hold values from -13 to 13
- value_states: bfloat16 [8192, 512], P(('groups', 'ctx'), 'head'), parts along dimension 0, may hold values from -6 to 6
- vertical: int32 [8, 2], P(('groups', 'head')), parts along dimension 0, may hold values from 0 to 31, as said below
- offsets: int32 [8, 4], P(('groups', 'head')), parts along dimension 0, may hold values from 0 to 960, as said below
Outputs:
- attended: bfloat16 [8192, 3584], P(('groups', 'ctx'), 'head'), parts along dimension 0
The draws below stay inside these ranges and needn't reach their ends.
There are 2 independent parts, one for each index of `groups`. The reference program is written for one: setup_inputs(seed, part) draws one part's arguments, and reference() takes and returns one part's arrays. A program takes and returns all parts, laid end to end along the dimension named above; each array names one. Nothing has to cross between parts.
Inputs may be any that keep to these rules, and one draw needn't show every extreme that they name: `vertical`: each row lists 2 distinct blocks; the 1024 tokens of one ctx shard hold at most one block of a row. `offsets`: each row holds distinct multiples of 64; its first entry is 0 and its second is 960.
All inputs are finite; a program needn't handle non-finite values.
Results may differ from the reference program's by a relative error of at most 0.0043.
Values may be sent and summed in bfloat16 or wider, within the bound.
No kernel may reach another device: no remote copies, remote signals or barrier semaphores. Data moves between devices by JAX's collectives and lax.ppermute only.
A program may use at most 256 MiB of HBM per device.

```python
import jax
import jax.numpy as jnp
from jax import lax

HEAD_DIM = 128
Q_HEADS = 28
KV_HEADS = 4
BLOCK = 128
BAND = 64
SLASH = 4
TOK_DEV = 1024
SEQ = 4096
VERT = 2
N_CTX = 4


def draw_queries(key, part):
    key = jax.random.fold_in(key, 11)
    result = jnp.clip(jax.random.normal(key, (SEQ, Q_HEADS * HEAD_DIM), jnp.float32), -6.0, 6.0)
    return result.astype(jnp.bfloat16)


def draw_key_states(key, part):
    key = jax.random.fold_in(key, 13)
    result = jnp.clip(jax.random.normal(key, (SEQ, KV_HEADS * HEAD_DIM), jnp.float32), -6.0, 6.0)
    return result.astype(jnp.bfloat16)


def draw_vertical(key, part):
    key = jax.random.fold_in(key, 21)
    per_shard = TOK_DEV // BLOCK

    def one_head(head_key):
        owner_key, pick_key = jax.random.split(head_key)
        owners = jax.random.permutation(owner_key, N_CTX)[:VERT]
        local_pick = jax.random.randint(pick_key, (VERT,), 0, per_shard)
        return (owners * per_shard + local_pick).astype(jnp.int32)
    return jax.vmap(one_head)(jax.random.split(key, KV_HEADS))


def draw_offsets(key, part):
    key = jax.random.fold_in(key, 31)
    steps_count = TOK_DEV // BAND

    def one_head(head_key):
        others = jax.random.permutation(head_key, steps_count - 2)[:SLASH - 2] + 1
        fixed = jnp.array([0, steps_count - 1], jnp.int32)
        return (jnp.concatenate([fixed, others.astype(jnp.int32)]) * BAND).astype(jnp.int32)
    return jax.vmap(one_head)(jax.random.split(key, KV_HEADS))


def block_levels(stream_key, dims, shards, smallest, top_value):
    loudness, own = 1.0, jax.random.fold_in(stream_key, 6)
    for position, shards_of in shards:
        steps = jnp.exp(jax.random.uniform(jax.random.fold_in(own, position), (shards_of,), jnp.float32, smallest / len(shards), top_value / len(shards)))
        loudness = loudness * jnp.repeat(steps, dims[position] // shards_of).reshape([-1 if axis == position else 1 for axis in range(len(dims))])
    return loudness


def noise(stream_key, shape, deviation, reach, pieces=(), kind=jnp.bfloat16):
    entries = deviation * jax.random.normal(stream_key, shape, jnp.float32)
    if pieces:
        entries = entries * block_levels(stream_key, shape, pieces, -0.22, 0.18)
    return jnp.clip(entries, -reach, reach).astype(kind)


def setup_inputs(seed: int = 0, part: int = 0) -> dict:
    arg_keys = jax.random.split(jax.random.key(seed), 6)
    part_keys = jax.random.split(jax.random.fold_in(arg_keys[5], part), 6)
    return {
        "queries": draw_queries(jax.random.fold_in(jax.random.fold_in(arg_keys[5], part), 71), part),
        "key_states": draw_key_states(jax.random.fold_in(jax.random.fold_in(arg_keys[5], part), 71), part),
        "value_states": noise(part_keys[2], (SEQ, KV_HEADS * HEAD_DIM), 1.0, 6.0, ((0, 4), (1, 4))),
        "vertical": draw_vertical(jax.random.fold_in(jax.random.fold_in(arg_keys[5], part), 71), part),
        "offsets": draw_offsets(jax.random.fold_in(jax.random.fold_in(arg_keys[5], part), 71), part),
    }


def reference(queries, key_states, value_states, vertical, offsets):
    group_size = Q_HEADS // KV_HEADS
    scaling = HEAD_DIM ** -0.5
    num_blocks = SEQ // BLOCK
    span = TOK_DEV + BLOCK
    results = []
    for head_idx in range(KV_HEADS):
        key_head = key_states[:, head_idx * HEAD_DIM:(head_idx + 1) * HEAD_DIM]
        value_head = value_states[:, head_idx * HEAD_DIM:(head_idx + 1) * HEAD_DIM]
        vert_list = vertical[head_idx].astype(jnp.int32)
        vert_keys = key_head.reshape(num_blocks, BLOCK, HEAD_DIM)[vert_list].reshape(VERT * BLOCK, HEAD_DIM)
        vert_vals = value_head.reshape(num_blocks, BLOCK, HEAD_DIM)[vert_list].reshape(VERT * BLOCK, HEAD_DIM)
        vert_pos = (vert_list[:, None] * BLOCK + jnp.arange(BLOCK, dtype=jnp.int32)[None, :]).reshape(-1)
        key_pad = jnp.concatenate([jnp.zeros((TOK_DEV, HEAD_DIM), key_head.dtype), key_head], 0)
        value_pad = jnp.concatenate([jnp.zeros((TOK_DEV, HEAD_DIM), value_head.dtype), value_head], 0)
        head_offs = offsets[head_idx].astype(jnp.int32)
        query_head = queries[:, head_idx * group_size * HEAD_DIM:(head_idx + 1) * group_size * HEAD_DIM]
        query_head = query_head.reshape(num_blocks, BLOCK, group_size, HEAD_DIM)

        def one_block(inputs, key_pad=key_pad, value_pad=value_pad, vert_keys=vert_keys,
                      vert_vals=vert_vals, vert_pos=vert_pos, vert_list=vert_list, head_offs=head_offs):
            query_block, block_idx = inputs
            first_row = block_idx * BLOCK
            query_pos = first_row + jnp.arange(BLOCK, dtype=jnp.int32)
            win_keys = lax.dynamic_slice_in_dim(key_pad, first_row, span, 0)
            win_vals = lax.dynamic_slice_in_dim(value_pad, first_row, span, 0)
            win_pos = first_row - TOK_DEV + jnp.arange(span, dtype=jnp.int32)
            distance = query_pos[:, None] - win_pos[None, :]
            in_band = jnp.any((distance[None] >= head_offs[:, None, None])
                              & (distance[None] < head_offs[:, None, None] + BAND), axis=0)
            in_vert = jnp.any((win_pos // BLOCK)[:, None] == vert_list[None, :], axis=1)
            win_mask = in_band & (win_pos >= 0)[None, :] & jnp.logical_not(in_vert)[None, :]
            vert_mask = vert_pos[None, :] <= query_pos[:, None]
            all_keys = jnp.concatenate([win_keys, vert_keys], 0)
            all_vals = jnp.concatenate([win_vals, vert_vals], 0)
            visible = jnp.concatenate([win_mask, vert_mask], 1)
            scores = jnp.einsum('tgd,kd->tgk', query_block.astype(jnp.float32), all_keys.astype(jnp.float32)) * scaling
            masked = jnp.where(visible[:, None, :], scores, -1e30)
            top = jnp.max(masked, axis=-1)
            weights = jnp.where(visible[:, None, :], jnp.exp(masked - top[..., None]), 0.0)
            total = jnp.sum(weights, axis=-1)
            rounded = weights.astype(jnp.bfloat16)
            summed = jnp.einsum('tgk,kd->tgd', rounded.astype(jnp.float32), all_vals.astype(jnp.float32))
            return (summed / total[..., None]).astype(jnp.bfloat16).reshape(BLOCK, group_size * HEAD_DIM)

        outputs = lax.map(one_block, (query_head, jnp.arange(num_blocks, dtype=jnp.int32)))
        results.append(outputs.reshape(SEQ, group_size * HEAD_DIM))
    return jnp.concatenate(results, axis=1)
```

```python
import functools
import math

import jax
import jax.numpy as jnp
from jax import lax
from jax.experimental import pallas as pl
from jax.experimental.pallas import tpu as pltpu
from jax.sharding import PartitionSpec as P

BLOCK = 128
BAND = 64
NEG = -1e30


def ring(block, axis, distance):
    size = lax.axis_size(axis)
    return lax.ppermute(block, axis, [(i, (i + distance) % size) for i in range(size)])


def listed_here(vertical, rank, per_shard):
    local = vertical[0] - rank * per_shard
    mine = (local >= 0) & (local < per_shard)
    return jnp.sum(jnp.where(mine, local, 0)) * BLOCK


def attention_kernel(offs, vert, q_hbm, k_own, v_own, k_prev, v_prev, *rest, heads, dim, unroll, direct):
    n_remote = len(rest) - 9
    remote, (o_hbm, q_buf, kw, vw, vk, vv, o_buf, sems, out_sems) = rest[:n_remote], rest[n_remote:]
    tok = k_own.shape[0]
    listed = vert.shape[1]
    bands = offs.shape[1]
    per_shard = tok // BLOCK
    steps = tok // BAND // unroll
    rows = unroll * BAND
    rank = lax.axis_index("ctx")
    scale = dim**-0.5 * math.log2(math.e)

    def fetch(src, dst, sem):
        return pltpu.make_async_copy(src, dst, sems.at[sem])

    loads = [
        fetch(k_own, kw.at[pl.ds(tok, tok), :], 0),
        fetch(k_prev, kw.at[pl.ds(0, tok), :], 1),
        fetch(v_own, vw.at[pl.ds(tok, tok), pl.ds(0, dim)], 2),
        fetch(v_prev, vw.at[pl.ds(0, tok), pl.ds(0, dim)], 3),
    ]
    for copy in loads:
        copy.start()
    q_sem = 4 + 2 * listed

    def q_copy(i):
        at = pl.ds(pl.multiple_of(i * rows, rows), rows)
        return fetch(q_hbm.at[at, :], q_buf.at[at, :], q_sem + i)

    for i in range(steps):
        q_copy(i).start()
    for v in range(listed):
        block = vert[0, v]
        owner = lax.div(block, per_shard)
        row = pl.multiple_of((block - owner * per_shard) * BLOCK, BLOCK)
        away = rank - owner
        k_dst, v_dst = vk.at[pl.ds(v * BLOCK, BLOCK), :], vv.at[pl.ds(v * BLOCK, BLOCK), pl.ds(0, dim)]
        sources = [(away <= 0, k_own.at[pl.ds(row, BLOCK), :], v_own.at[pl.ds(row, BLOCK), :])]
        sources += [(away == 1, k_prev.at[pl.ds(row, BLOCK), :], v_prev.at[pl.ds(row, BLOCK), :])]
        if direct:
            sources += [
                (away == 2 + i, r.at[pl.ds(0, BLOCK), :], r.at[pl.ds(BLOCK, BLOCK), :])
                for i, r in enumerate(remote)
            ]
        else:
            (r,) = remote
            at = pl.multiple_of(owner * 2 * BLOCK, BLOCK)
            sources += [(away >= 2, r.at[pl.ds(at, BLOCK), :], r.at[pl.ds(at + BLOCK, BLOCK), :])]
        for here, k_src, v_src in sources:

            @pl.when(here)
            def _():
                fetch(k_src, k_dst, 4 + 2 * v).start()
                fetch(v_src, v_dst, 5 + 2 * v).start()

    vw[:, dim:] = jnp.ones((2 * tok, dim), jnp.bfloat16)
    vv[:, dim:] = jnp.ones((listed * BLOCK, dim), jnp.bfloat16)
    r_at = lax.broadcasted_iota(jnp.int32, (BAND, BLOCK), 0)
    t_at = lax.broadcasted_iota(jnp.int32, (BAND, BLOCK), 1)
    band_bias = jnp.where((t_at > r_at) & (t_at <= r_at + BAND), 0.0, NEG)
    low = t_at < BAND
    for copy in loads:
        copy.wait()
    for v in range(listed):
        fetch(k_own.at[pl.ds(0, BLOCK), :], vk.at[pl.ds(v * BLOCK, BLOCK), :], 4 + 2 * v).wait()
        fetch(v_own.at[pl.ds(0, BLOCK), :], vv.at[pl.ds(v * BLOCK, BLOCK), pl.ds(0, dim)], 5 + 2 * v).wait()
    first = rank * (tok // BAND)

    def row_block(a):
        at = pl.ds(pl.multiple_of(a * BAND, BAND), BAND)
        q = jnp.concatenate([q_buf[at, h * dim : (h + 1) * dim] for h in range(heads)], 0)
        keys, values, biases = [], [], []
        for s in range(bands):
            back = lax.div(offs[0, s], BAND)
            start = pl.multiple_of(tok + (a - back - 1) * BAND, BAND)
            keys.append(kw[pl.ds(start, BLOCK), :])
            values.append(vw[pl.ds(start, BLOCK), :])
            column = []
            for half in (first + a - back - 1, first + a - back):
                hidden = half < 0
                for v in range(listed):
                    hidden = hidden | (lax.shift_right_arithmetic(half, 1) == vert[0, v])
                column.append(jnp.where(hidden, jnp.float32(NEG), jnp.float32(0)))
            biases.append(band_bias + jnp.where(low, column[0], column[1]))
        for v in range(listed):
            reach = (first + a) * BAND - vert[0, v] * BLOCK
            biases.append(jnp.where(t_at <= r_at + reach, 0.0, NEG))
        keys = jnp.concatenate(keys + [vk[...]], 0)
        values = jnp.concatenate(values + [vv[...]], 0)
        scores = lax.dot_general(q, keys, (((1,), (1,)), ((), ())), preferred_element_type=jnp.float32)
        parts = [
            scores[:, i * BLOCK : (i + 1) * BLOCK].reshape(heads, BAND, BLOCK) + bias[None]
            for i, bias in enumerate(biases)
        ]
        top = jnp.max(functools.reduce(jnp.maximum, parts), axis=-1, keepdims=True)
        weights = [
            jnp.exp2((part - top) * scale).reshape(heads * BAND, BLOCK).astype(jnp.bfloat16) for part in parts
        ]
        acc = jnp.dot(jnp.concatenate(weights, 1), values, preferred_element_type=jnp.float32)
        out = acc[:, :dim] / acc[:, dim:]
        for h in range(heads):
            o_buf[at, h * dim : (h + 1) * dim] = out[h * BAND : (h + 1) * BAND].astype(jnp.bfloat16)

    def o_copy(i):
        at = pl.ds(pl.multiple_of(i * rows, rows), rows)
        return pltpu.make_async_copy(o_buf.at[at, :], o_hbm.at[at, :], out_sems.at[i])

    def step(i, carry):
        q_copy(i).wait()
        for u in range(unroll):
            row_block(i * unroll + u)
        o_copy(i).start()
        return carry

    lax.fori_loop(0, steps, step, 0)
    for i in range(steps):
        o_copy(i).wait()


def per_device(queries, key_states, value_states, vertical, offsets):
    tok, dim = key_states.shape
    heads = queries.shape[1] // dim
    listed = vertical.shape[1]
    n_ctx = lax.axis_size("ctx")
    rank = lax.axis_index("ctx")
    k_prev, v_prev = ring(key_states, "ctx", 1), ring(value_states, "ctx", 1)
    row = listed_here(vertical, rank, tok // BLOCK)
    mine = jnp.concatenate(
        [lax.dynamic_slice_in_dim(x, row, BLOCK, 0) for x in (key_states, value_states)], 0
    )
    direct = n_ctx <= 4
    if direct:
        remote = [ring(mine, "ctx", d) for d in range(2, n_ctx)]
    else:
        remote = [lax.all_gather(mine, "ctx", axis=0, tiled=True)]
    unroll = 4
    steps = tok // BAND // unroll
    smem, hbm = pl.BlockSpec(memory_space=pltpu.SMEM), pl.BlockSpec(memory_space=pl.ANY)
    return pl.pallas_call(
        functools.partial(attention_kernel, heads=heads, dim=dim, unroll=unroll, direct=direct),
        out_shape=jax.ShapeDtypeStruct(queries.shape, jnp.bfloat16),
        in_specs=[smem] * 2 + [hbm] * (5 + len(remote)),
        out_specs=hbm,
        scratch_shapes=[
            pltpu.VMEM(queries.shape, jnp.bfloat16),
            pltpu.VMEM((2 * tok, dim), jnp.bfloat16),
            pltpu.VMEM((2 * tok, 2 * dim), jnp.bfloat16),
            pltpu.VMEM((listed * BLOCK, dim), jnp.bfloat16),
            pltpu.VMEM((listed * BLOCK, 2 * dim), jnp.bfloat16),
            pltpu.VMEM(queries.shape, jnp.bfloat16),
            pltpu.SemaphoreType.DMA((4 + 2 * listed + steps,)),
            pltpu.SemaphoreType.DMA((steps,)),
        ],
        compiler_params=pltpu.CompilerParams(vmem_limit_bytes=40 * 2**20),
    )(offsets, vertical, queries, key_states, value_states, k_prev, v_prev, *remote)


def solution(mesh):
    placed = (
        P(("groups", "ctx"), "head"),
        P(("groups", "ctx"), "head"),
        P(("groups", "ctx"), "head"),
        P(("groups", "head"), None),
        P(("groups", "head"), None),
    )
    return jax.shard_map(
        per_device,
        mesh=mesh,
        in_specs=placed,
        out_specs=P(("groups", "ctx"), "head"),
        check_vma=False,
    )
```

```python
import functools
import math

import jax
import jax.numpy as jnp
from jax import lax
from jax.experimental import pallas as pl
from jax.experimental.pallas import tpu as pltpu
from jax.sharding import PartitionSpec as P

BLOCK = 128
BAND = 64
NEG = -1e30
UNROLL = 4
OWN_UNROLL = 8


def ring(block, axis, distance):
    size = lax.axis_size(axis)
    return lax.ppermute(block, axis, [(i, (i + distance) % size) for i in range(size)])


def sorted_backs(offs):
    a, b = lax.div(offs[0, 2], BAND), lax.div(offs[0, 3], BAND)
    return lax.div(offs[0, 0], BAND), jnp.minimum(a, b), jnp.maximum(a, b), lax.div(offs[0, 1], BAND)


def band_mask():
    r = lax.broadcasted_iota(jnp.int32, (BAND, BLOCK), 0)
    t = lax.broadcasted_iota(jnp.int32, (BAND, BLOCK), 1)
    return r, t, jnp.where((t > r) & (t <= r + BAND), 0.0, NEG)


def is_listed(half, vert):
    found = lax.shift_right_arithmetic(half, 1) == vert[0, 0]
    for v in range(1, vert.shape[1]):
        found = found | (lax.shift_right_arithmetic(half, 1) == vert[0, v])
    return found


def bias_of(hidden, mask, t_at):
    low, high = (jnp.where(h, jnp.float32(NEG), jnp.float32(0)) for h in hidden)
    return mask + jnp.where(t_at < BAND, low, high)


def two_halves(ref, first, second):
    at = [pl.ds(pl.multiple_of(h * BAND, BAND), BAND) for h in (first, second)]
    return [ref[at[0], :], ref[at[1], :]]


def stacked(q_ref, a, heads, dim):
    at = pl.ds(pl.multiple_of(a * BAND, BAND), BAND)
    return jnp.concatenate([q_ref[at, h * dim : (h + 1) * dim] for h in range(heads)], 0)


def scores_of(q, keys, biases, heads):
    scores = lax.dot_general(q, keys, (((1,), (1,)), ((), ())), preferred_element_type=jnp.float32)
    return [
        (scores[:, i * BLOCK : (i + 1) * BLOCK].reshape(heads, BAND, BLOCK) + bias[None]).reshape(
            heads * BAND, BLOCK
        )
        for i, bias in enumerate(biases)
    ]


def row_max(parts):
    return jnp.max(functools.reduce(jnp.maximum, parts), axis=-1, keepdims=True)


def write_all(stores):
    for ref, index, value in stores:
        ref[index] = value


def run_stages(bodies):
    order = [(0, 0)]
    for u in range(len(bodies)):
        order += [(u + 1, 0)] * (u + 1 < len(bodies)) + [(u, 1), (u, 2)]
    write_all([store for u, _ in order for store in next(bodies[u]) or []])


def unrolled(count, body, unroll, start=0, after=None):
    def step(i, carry):
        run_stages([body(i * unroll + u) for u in range(unroll)])
        if after is not None:
            after(i)
        return carry

    lax.fori_loop(start // unroll, count // unroll, step, 0)


def with_ones(values):
    return jnp.concatenate([values, jnp.ones_like(values)], 1)


def move_all(copies, sems):
    copies = [pltpu.make_async_copy(src, dst, sems.at[i]) for i, (src, dst) in enumerate(copies)]
    for copy in copies:
        copy.start()
    for copy in copies:
        copy.wait()


def own_listed(vert, rank, per_shard):
    block = jnp.int32(-1)
    for v in range(vert.shape[1]):
        local = vert[0, v] - rank * per_shard
        block = jnp.where((local >= 0) & (local < per_shard), local, block)
    return block


def block_at(block):
    return pl.ds(pl.multiple_of(block * BLOCK, BLOCK), BLOCK)


def pick_kernel(vert_hbm, k_hbm, v_hbm, mine, vert, sems):
    move_all([(vert_hbm, vert)], sems)
    block = own_listed(vert, lax.axis_index("ctx"), k_hbm.shape[0] // BLOCK)
    at = block_at(jnp.maximum(block, 0))
    move_all([(x.at[at, :], mine.at[pl.ds(i * BLOCK, BLOCK), :]) for i, x in enumerate((k_hbm, v_hbm))], sems)


def own_kernel(offs, vert, q_ref, k_own, v_own, acc_ref, top_ref, *, heads, dim):
    tok = k_own.shape[0]
    rows = heads * BAND
    rank = lax.axis_index("ctx")
    first = rank * (tok // BAND)
    scale = dim**-0.5 * math.log2(math.e)
    r_at, t_at, mask = band_mask()
    backs = sorted_backs(offs)[:3]
    listed = own_listed(vert, rank, tok // BLOCK)
    listed_at = block_at(jnp.maximum(listed, 0))
    listed_from = jnp.where(listed < 0, tok, listed * BLOCK)

    def row_block(a):
        keys, values, biases = [], [], []
        for back in backs:
            halves = (a - back - 1, a - back)
            rows_at = [jnp.maximum(h, 0) for h in halves]
            keys += two_halves(k_own, *rows_at)
            values += two_halves(v_own, *rows_at)
            biases.append(bias_of([(h < 0) | is_listed(first + h, vert) for h in halves], mask, t_at))
        biases.append(jnp.where(t_at - r_at <= a * BAND - listed_from, 0.0, NEG))
        q = stacked(q_ref, a, heads, dim)
        parts = scores_of(q, jnp.concatenate(keys + [k_own[listed_at, :]], 0), biases, heads)
        yield
        top = row_max(parts)
        rounded = jnp.concatenate([jnp.exp2((x - top) * scale).astype(jnp.bfloat16) for x in parts], 1)
        yield
        values = with_ones(jnp.concatenate(values + [v_own[listed_at, :]], 0))
        acc = jnp.dot(rounded, values, preferred_element_type=jnp.float32)
        at = pl.ds(pl.multiple_of(a * rows, rows), rows)
        yield [(acc_ref, (at, slice(None)), acc), (top_ref, (at, slice(None)), jnp.broadcast_to(top, (rows, BLOCK)))]

    unrolled(tok // BAND, row_block, OWN_UNROLL)


def band_rows(prev, own, a, back, per_half, last):
    low, high = two_halves(prev, *[jnp.minimum(a - back - e + per_half, per_half - 1) for e in (1, 0)])
    if last:
        high = jnp.where(a == back, own[0:BAND, :], high)
    return [low, high]


def rest_kernel(offs, vert, q_ref, k_own, v_own, acc_ref, top_ref, k_prev, v_prev, *rest, heads, dim, direct):
    remote, (o_hbm, vk, vv, o_buf, sems) = rest[:-5], rest[-5:]
    tok = k_own.shape[0]
    rows = heads * BAND
    per_shard = tok // BLOCK
    per_half = tok // BAND
    rank = lax.axis_index("ctx")
    first = rank * per_half
    scale = dim**-0.5 * math.log2(math.e)
    listed = vert.shape[1]
    unroll = UNROLL if listed <= 4 else 1

    def out_copy(i):
        at = pl.ds(pl.multiple_of(i * unroll * BAND, unroll * BAND), unroll * BAND)
        return pltpu.make_async_copy(o_buf.at[at, :], o_hbm.at[at, :], sems.at[i])

    def result(a, acc):
        out = (acc[:, :dim] / acc[:, dim:]).astype(jnp.bfloat16)
        to = pl.ds(pl.multiple_of(a * BAND, BAND), BAND)
        return [(o_buf, (to, slice(h * dim, (h + 1) * dim)), out[h * BAND : (h + 1) * BAND]) for h in range(heads)]

    _, t_at, mask = band_mask()
    backs = sorted_backs(offs)
    hidden_block = []
    for v in range(listed):
        block = vert[0, v]
        owner = lax.div(block, per_shard)
        row = pl.multiple_of((block - owner * per_shard) * BLOCK, BLOCK)
        away = rank - owner
        hidden_block.append(jnp.where(away > 0, jnp.float32(0), jnp.float32(NEG)))
        slot = pl.ds(v * BLOCK, BLOCK)
        sources = [(away <= 0, k_own, row, v_own, row), (away == 1, k_prev, row, v_prev, row)]
        if direct:
            sources += [(away == 2 + i, x, 0, x, BLOCK) for i, x in enumerate(remote)]
        else:
            at = pl.multiple_of(owner * 2 * BLOCK, BLOCK)
            sources += [(away >= 2, remote[0], at, remote[0], at + BLOCK)]
        for here, k_src, k_row, v_src, v_row in sources:

            @pl.when(here)
            def _():
                vk[slot, :] = k_src[pl.ds(k_row, BLOCK), :]
                vv[slot, :] = v_src[pl.ds(v_row, BLOCK), :]

    def row_block(a, backs):
        keys, values, biases = [], [], []
        for i, back in enumerate(backs):
            last = i == len(backs) - 1
            keys += band_rows(k_prev, k_own, a, back, per_half, last)
            values += band_rows(v_prev, v_own, a, back, per_half, last)
            low, high = a - back - 1, a - back
            hidden = [
                (low >= 0) | (first + low < 0) | is_listed(first + low, vert),
                (high > 0 if last else high >= 0) | (first + high < 0) | is_listed(first + high, vert),
            ]
            biases.append(bias_of(hidden, mask, t_at))
        biases += [jnp.full((BAND, BLOCK), b) for b in hidden_block]
        at = pl.ds(pl.multiple_of(a * rows, rows), rows)
        q = stacked(q_ref, a, heads, dim)
        parts = scores_of(q, jnp.concatenate(keys + [vk[...]], 0), biases, heads)
        yield
        own_top = top_ref[at, :]
        top = jnp.maximum(row_max(parts), own_top)
        rounded = jnp.concatenate([jnp.exp2((x - top) * scale).astype(jnp.bfloat16) for x in parts], 1)
        own = jnp.exp2((own_top - top) * scale)
        yield
        values = with_ones(jnp.concatenate(values + [vv[...]], 0))
        acc = jnp.dot(rounded, values, preferred_element_type=jnp.float32)
        yield result(a, acc + jnp.concatenate([own, own], 1) * acc_ref[at, :])

    def group(i, backs):
        start = len(backs) - 3
        run_stages(
            [
                row_block(i * unroll + u, backs if u == 0 and start == 1 else backs[max(start, 0) :])
                for u in range(unroll)
            ]
        )

    def step(i, carry):
        @pl.when(i * unroll <= backs[1])
        def _():
            group(i, backs)

        @pl.when(i * unroll > backs[1])
        def _():
            group(i, backs[2:])

        out_copy(i).start()
        return carry

    def first_step(i, carry):
        for u in range(unroll):
            a = i * unroll + u
            write_all(result(a, acc_ref[pl.ds(pl.multiple_of(a * rows, rows), rows), :]))

        @pl.when(i == per_half // unroll - 1)
        def _():
            run_stages([row_block(per_half - 1, backs[3:])])

        out_copy(i).start()
        return carry

    @pl.when(rank == 0)
    def _():
        lax.fori_loop(0, per_half // unroll, first_step, 0)

    @pl.when(rank > 0)
    def _():
        lax.fori_loop(0, per_half // unroll, step, 0)

    for i in range(per_half // unroll):
        out_copy(i).wait()


def per_device(queries, key_states, value_states, vertical, offsets):
    tok, dim = key_states.shape
    heads = queries.shape[1] // dim
    listed = vertical.shape[1]
    n_ctx = lax.axis_size("ctx")
    all_rows = tok * heads
    smem, vmem, hbm = (pl.BlockSpec(memory_space=m) for m in (pltpu.SMEM, pltpu.VMEM, pltpu.HBM))
    f32, bf16 = jnp.float32, jnp.bfloat16

    def params(flops, limit=16):
        return dict(
            compiler_params=pltpu.CompilerParams(vmem_limit_bytes=limit * 2**20),
            cost_estimate=pl.CostEstimate(flops=flops, bytes_accessed=2**20, transcendentals=0),
        )

    k_prev, v_prev = ring(key_states, "ctx", 1), ring(value_states, "ctx", 1)
    mine = pl.pallas_call(
        pick_kernel,
        out_shape=jax.ShapeDtypeStruct((2 * BLOCK, dim), bf16),
        in_specs=[hbm] * 3,
        out_specs=vmem,
        scratch_shapes=[pltpu.SMEM(vertical.shape, jnp.int32), pltpu.SemaphoreType.DMA((2,))],
        **params(10**6, 60),
    )(vertical, key_states, value_states)
    direct = n_ctx <= 4
    if direct:
        remote = [ring(mine, "ctx", d) for d in range(2, n_ctx)]
    else:
        remote = [lax.all_gather(mine, "ctx", axis=0, tiled=True)]
    acc1, top = pl.pallas_call(
        functools.partial(own_kernel, heads=heads, dim=dim),
        out_shape=[
            jax.ShapeDtypeStruct((all_rows, 2 * dim), f32),
            jax.ShapeDtypeStruct((all_rows, BLOCK), f32),
        ],
        in_specs=[smem, smem, vmem, vmem, vmem],
        out_specs=[vmem] * 2,
        **params(10**6, 24),
    )(offsets, vertical, queries, key_states, value_states)
    unroll = UNROLL if listed <= 4 else 1
    return pl.pallas_call(
        functools.partial(rest_kernel, heads=heads, dim=dim, direct=direct),
        out_shape=jax.ShapeDtypeStruct(queries.shape, bf16),
        in_specs=[smem, smem] + [vmem] * (7 + len(remote)),
        out_specs=hbm,
        scratch_shapes=[pltpu.VMEM((listed * BLOCK, dim), bf16)] * 2
        + [
            pltpu.VMEM(queries.shape, bf16),
            pltpu.SemaphoreType.DMA((tok // BAND // unroll,)),
        ],
        **params(10**6, 24),
    )(offsets, vertical, queries, key_states, value_states, acc1, top, k_prev, v_prev, *remote)


def solution(mesh):
    placed = (
        P(("groups", "ctx"), "head"),
        P(("groups", "ctx"), "head"),
        P(("groups", "ctx"), "head"),
        P(("groups", "head"), None),
        P(("groups", "head"), None),
    )
    return jax.shard_map(
        per_device,
        mesh=mesh,
        in_specs=placed,
        out_specs=P(("groups", "ctx"), "head"),
        check_vma=False,
    )
```

```python
import functools
import math

import jax
import jax.numpy as jnp
from jax import lax
from jax.experimental import pallas as pl
from jax.experimental.pallas import tpu as pltpu
from jax.sharding import PartitionSpec as P

BLOCK = 128
BAND = 64
CHUNK = 2
NEG = -1e30


def ring(block, axis, distance):
    size = lax.axis_size(axis)
    return lax.ppermute(block, axis, [(i, (i + distance) % size) for i in range(size)])


def line(block, axis, distance):
    size = lax.axis_size(axis)
    return lax.ppermute(block, axis, [(i, i + distance) for i in range(size - distance)])


def start_all(copies):
    for copy in copies:
        copy.start()


def wait_all(copies):
    for copy in copies:
        copy.wait()


def copies_of(pairs, sems):
    return [pltpu.make_async_copy(src, dst, sems.at[i]) for i, (src, dst) in enumerate(pairs)]


def block_at(block):
    return pl.ds(pl.multiple_of(block * BLOCK, BLOCK), BLOCK)


def listed_in(vert, shard, per_shard):
    block = jnp.int32(-1)
    for v in range(vert.shape[1]):
        local = vert[0, v] - shard * per_shard
        block = jnp.where((local >= 0) & (local < per_shard), local, block)
    return block


def early_block(vert, shard, per_shard):
    listed = listed_in(vert, shard, per_shard)
    half = per_shard // 2
    return jnp.where((listed >= 0) & (listed < half), listed, half - 1)


def late_block(early, j):
    return jnp.where(j >= early, j + 1, j)


def is_listed(half, vert):
    found = lax.shift_right_arithmetic(half, 1) == vert[0, 0]
    for v in range(1, vert.shape[1]):
        found = found | (lax.shift_right_arithmetic(half, 1) == vert[0, v])
    return found


def run_stages(bodies, after):
    order = [(0, 0)]
    for u in range(len(bodies)):
        order += [(u + 1, 0)] * (u + 1 < len(bodies)) + [(u, 1), (u, 2)]
    done = 0
    for u, _ in order:
        stores = next(bodies[u]) or []
        for ref, index, value in stores:
            ref[index] = value
        if stores:
            done += 1
            after(done)


def pick_kernel(vert_hbm, k_hbm, v_hbm, mine, early, vert, sems):
    load = copies_of([(vert_hbm, vert)], sems)
    start_all(load)
    tok = k_hbm.shape[0]
    per_shard = tok // BLOCK
    half = per_shard // 2
    rank = lax.axis_index("ctx")
    upper = pl.ds(tok // 2, tok // 2)
    pairs = []
    for i, x in enumerate((k_hbm, v_hbm)):
        pairs.append((x.at[upper, :], early.at[pl.ds(i * (half + 1) * BLOCK, half * BLOCK), :]))
    first = copies_of(pairs, sems.at[pl.ds(1, 2)])
    start_all(first)
    wait_all(load)
    listed = jnp.maximum(listed_in(vert, rank, per_shard), 0)
    moved = early_block(vert, rank, per_shard)
    pairs = []
    for i, x in enumerate((k_hbm, v_hbm)):
        pairs.append((x.at[block_at(listed), :], mine.at[pl.ds(i * BLOCK, BLOCK), :]))
        pairs.append((x.at[block_at(moved), :], early.at[pl.ds((i * (half + 1) + half) * BLOCK, BLOCK), :]))
    second = copies_of(pairs, sems.at[pl.ds(3, len(pairs))])
    start_all(second)
    wait_all(first + second)


def load_kernel(vert, offs_hbm, q_hbm, k_hbm, v_hbm, late, offs, q_ref, kw, vw, sems):
    tok = k_hbm.shape[0]
    per_shard = tok // BLOCK
    half = per_shard // 2
    own = pl.ds(tok, tok)
    moved = early_block(vert, lax.axis_index("ctx"), per_shard)
    pairs = [
        (x.at[block_at(late_block(moved, j)), :], late.at[pl.ds((i * (half - 1) + j) * BLOCK, BLOCK), :])
        for i, x in enumerate((k_hbm, v_hbm))
        for j in range(half - 1)
    ]
    pairs += [(offs_hbm, offs), (k_hbm, kw.at[own, :]), (v_hbm, vw.at[own, :]), (q_hbm, q_ref)]
    loads = copies_of(pairs, sems)
    start_all(loads)

    @pl.when(lax.axis_index("ctx") == 0)
    def _():
        zero = jnp.zeros((tok, k_hbm.shape[1]), jnp.bfloat16)
        kw[pl.ds(0, tok), :] = zero
        vw[pl.ds(0, tok), :] = zero

    wait_all(loads)


def attend_rows(groups, unroll, base, o_hbm, offs, vert, q_ref, kw, vw, vk, vv, o_buf, o_sems, heads, dim):
    tok = q_ref.shape[0]
    rows = heads * BAND
    listed = vert.shape[1]
    first = lax.axis_index("ctx") * (tok // BAND)
    scale = dim**-0.5 * math.log2(math.e)
    group = unroll * BAND
    r_at = lax.broadcasted_iota(jnp.int32, (BAND, BLOCK), 0)
    t_at = lax.broadcasted_iota(jnp.int32, (BAND, BLOCK), 1)
    mask = jnp.where((t_at > r_at) & (t_at <= r_at + BAND), 0.0, NEG)

    def row_block(a):
        keys, values, biases = [], [], []
        for s in range(offs.shape[1]):
            low = a - lax.div(offs[0, s], BAND) - 1
            at = pl.ds(pl.multiple_of(tok + low * BAND, BAND), BLOCK)
            keys.append(kw[at, :])
            values.append(vw[at, :])
            hidden = [(first + h < 0) | is_listed(first + h, vert) for h in (low, low + 1)]
            column = [jnp.where(h, jnp.float32(NEG), jnp.float32(0)) for h in hidden]
            biases.append(mask + jnp.where(t_at < BAND, column[0], column[1]))
        for v in range(listed):
            reach = (first + a) * BAND - vert[0, v] * BLOCK
            biases.append(jnp.where(t_at - r_at <= reach, 0.0, NEG))
        at = pl.ds(pl.multiple_of(a * BAND, BAND), BAND)
        q = jnp.concatenate([q_ref[at, h * dim : (h + 1) * dim] for h in range(heads)], 0)
        keys = jnp.concatenate(keys + [vk[...]], 0)
        scores = lax.dot_general(q, keys, (((1,), (1,)), ((), ())), preferred_element_type=jnp.float32)
        parts = [
            (scores[:, i * BLOCK : (i + 1) * BLOCK].reshape(heads, BAND, BLOCK) + bias[None]).reshape(rows, BLOCK)
            for i, bias in enumerate(biases)
        ]
        yield
        top = jnp.max(functools.reduce(jnp.maximum, parts), axis=-1, keepdims=True)
        rounded = jnp.concatenate([jnp.exp2((x - top) * scale).astype(jnp.bfloat16) for x in parts], 1)
        yield
        values = jnp.concatenate(values + [vv[...]], 0)
        values = jnp.concatenate([values, jnp.ones_like(values)], 1)
        acc = jnp.dot(rounded, values, preferred_element_type=jnp.float32)
        out = (acc[:, :dim] / acc[:, dim:]).astype(jnp.bfloat16)
        yield [(o_buf, (at, slice(h * dim, (h + 1) * dim)), out[h * BAND : (h + 1) * BAND]) for h in range(heads)]

    chunk = min(unroll, CHUNK)

    def out_copy(c):
        at = pl.ds(pl.multiple_of((base + c * chunk) * BAND, chunk * BAND), chunk * BAND)
        return pltpu.make_async_copy(o_buf.at[at, :], o_hbm.at[at, :], o_sems.at[c])

    def step(g, carry):
        def after(done):
            if done % chunk == 0:
                out_copy(g * (unroll // chunk) + done // chunk - 1).start()

        run_stages([row_block(base + g * unroll + u) for u in range(unroll)], after)
        return carry

    lax.fori_loop(0, groups, step, 0)
    for c in range(groups * unroll // chunk):
        out_copy(c).wait()


def load_listed(vert, rank, k_own, v_own, vk, vv, others):
    per_shard = k_own.shape[0] // BLOCK
    for v in range(vert.shape[1]):
        owner = lax.div(vert[0, v], per_shard)
        local = vert[0, v] - owner * per_shard
        dst = pl.ds(v * BLOCK, BLOCK)
        for here, k_src, v_src, k_block, v_block in [
            (rank <= owner, k_own, v_own, local, local),
            *others(owner, local),
        ]:

            @pl.when(here)
            def _():
                vk[dst, :] = k_src[block_at(k_block), :]
                vv[dst, :] = v_src[block_at(v_block), :]


def first_kernel(offs, vert, q_ref, k_win, v_win, o_hbm, vk, vv, o_buf, o_sems, *, heads, dim, unroll):
    tok = q_ref.shape[0]
    own = pl.ds(tok, tok)
    rank = lax.axis_index("ctx")

    @pl.when(rank == 0)
    def _():
        load_listed(vert, rank, k_win.at[own, :], v_win.at[own, :], vk, vv, lambda owner, local: [])
        attend_rows(
            tok // BAND // unroll, unroll, 0, o_hbm, offs, vert, q_ref, k_win, v_win, vk, vv, o_buf, o_sems, heads, dim
        )


def upper_kernel(offs, vert, q_ref, early, *refs, heads, dim, direct, unroll):
    remote, (o_hbm, kw, vw, vk, vv, o_buf, o_sems) = refs[:-10][::-1], refs[-7:]
    tok = q_ref.shape[0]
    per_shard = tok // BLOCK
    half = per_shard // 2
    rank = lax.axis_index("ctx")

    @pl.when(rank > 0)
    def _():
        moved = early_block(vert, rank - 1, per_shard)
        for i, w in enumerate((kw, vw)):
            at = i * (half + 1) * BLOCK
            w[pl.ds(half * BLOCK, half * BLOCK), :] = early[pl.ds(at, half * BLOCK), :]
            w[block_at(moved), :] = early[pl.ds(at + half * BLOCK, BLOCK), :]

        def others(owner, local):
            found = [(rank == owner + 1, kw, vw, local, local)]
            if direct:
                found += [(rank == owner + 2 + i, x, x, 0, 1) for i, x in enumerate(remote)]
            else:
                found.append((rank >= owner + 2, remote[0], remote[0], 2 * owner, 2 * owner + 1))
            return found

        own = pl.ds(tok, tok)
        load_listed(vert, rank, kw.at[own, :], vw.at[own, :], vk, vv, others)
        n = tok // BAND // 2
        attend_rows(n // unroll, unroll, n, o_hbm, offs, vert, q_ref, kw, vw, vk, vv, o_buf, o_sems, heads, dim)


def lower_kernel(offs, vert, q_ref, late, vk, vv, _o, _kw, _vw, o_hbm, kw, vw, o_buf, o_sems, *, heads, dim, unroll):
    tok = q_ref.shape[0]
    per_shard = tok // BLOCK
    half = per_shard // 2
    rank = lax.axis_index("ctx")

    @pl.when(rank > 0)
    def _():
        moved = early_block(vert, rank - 1, per_shard)
        for i, w in enumerate((kw, vw)):
            for j in range(half - 1):
                w[block_at(late_block(moved, j)), :] = late[pl.ds((i * (half - 1) + j) * BLOCK, BLOCK), :]
        n = tok // BAND // 2
        attend_rows(n // unroll, unroll, 0, o_hbm, offs, vert, q_ref, kw, vw, vk, vv, o_buf, o_sems, heads, dim)


def per_device(queries, key_states, value_states, vertical, offsets):
    tok, dim = key_states.shape
    heads = queries.shape[1] // dim
    listed = vertical.shape[1]
    n_ctx = lax.axis_size("ctx")
    half = tok // BLOCK // 2
    bf16 = jnp.bfloat16
    hbm = pl.BlockSpec(memory_space=pl.ANY)
    pinned = [
        pltpu.with_memory_space_constraint(x, pltpu.HBM)
        for x in (offsets, vertical, queries, key_states, value_states)
    ]
    vmem, smem = pl.BlockSpec(memory_space=pltpu.VMEM), pl.BlockSpec(memory_space=pltpu.SMEM)

    def params(flops, limit=24):
        return dict(
            compiler_params=pltpu.CompilerParams(vmem_limit_bytes=limit * 2**20),
            cost_estimate=pl.CostEstimate(flops=flops, bytes_accessed=2**20, transcendentals=0),
        )

    window, blocks = (2 * tok, dim), (listed * BLOCK, dim)
    mine, early, vert = pl.pallas_call(
        pick_kernel,
        out_shape=[pltpu.VMEM((2 * n * BLOCK, dim), bf16) for n in (1, half + 1)]
        + [pltpu.SMEM(vertical.shape, jnp.int32)],
        in_specs=[hbm] * 3,
        out_specs=[vmem, vmem, smem],
        scratch_shapes=[pltpu.SemaphoreType.DMA((7,))],
        **params(10**6),
    )(pinned[1], pinned[3], pinned[4])
    early = ring(early, "ctx", 1)
    direct = n_ctx <= 4
    if direct:
        remote = [line(mine, "ctx", d) for d in range(2, n_ctx)]
    else:
        remote = [lax.all_gather(mine, "ctx", axis=0, tiled=True)]
    late, offs, q, kw, vw = pl.pallas_call(
        load_kernel,
        out_shape=[
            pltpu.VMEM((2 * (half - 1) * BLOCK, dim), bf16),
            pltpu.SMEM(offsets.shape, jnp.int32),
            pltpu.VMEM(queries.shape, bf16),
            pltpu.VMEM(window, bf16),
            pltpu.VMEM(window, bf16),
        ],
        in_specs=[smem] + [hbm] * 4,
        out_specs=[vmem, smem, vmem, vmem, vmem],
        scratch_shapes=[pltpu.SemaphoreType.DMA((2 * half + 2,))],
        **params(10**6),
    )(vert, pinned[0], *pinned[2:])
    late = ring(late, "ctx", 1)
    unroll = (4, 8, 8) if listed <= 4 else (1, 1, 1)
    o_shape = jax.ShapeDtypeStruct(queries.shape, bf16)
    buffers = [pltpu.VMEM(queries.shape, bf16)]
    done = [pltpu.SemaphoreType.DMA((tok // BAND,))]
    out = pl.pallas_call(
        functools.partial(first_kernel, heads=heads, dim=dim, unroll=unroll[0]),
        out_shape=o_shape,
        in_specs=[smem, smem] + [vmem] * 3,
        out_specs=hbm,
        scratch_shapes=[pltpu.VMEM(blocks, bf16)] * 2 + buffers + done,
        **params(FLOPS[0]),
    )(offs, vert, q, kw, vw)
    n = 4 + len(remote)
    out, kw, vw, vk, vv = pl.pallas_call(
        functools.partial(upper_kernel, heads=heads, dim=dim, direct=direct, unroll=unroll[1]),
        out_shape=[o_shape] + [pltpu.VMEM(x, bf16) for x in (window, window, blocks, blocks)],
        in_specs=[smem, smem, vmem, vmem] + [vmem] * len(remote) + [hbm, vmem, vmem],
        out_specs=[hbm] + [vmem] * 4,
        input_output_aliases={n: 0, n + 1: 1, n + 2: 2},
        scratch_shapes=buffers + done,
        **params(FLOPS[1]),
    )(offs, vert, q, early, *remote[::-1], out, kw, vw)
    out, _, _ = pl.pallas_call(
        functools.partial(lower_kernel, heads=heads, dim=dim, unroll=unroll[2]),
        out_shape=[o_shape] + [pltpu.VMEM(window, bf16)] * 2,
        in_specs=[smem, smem] + [vmem] * 4 + [hbm, vmem, vmem],
        out_specs=[hbm] + [vmem] * 2,
        input_output_aliases={6: 0, 7: 1, 8: 2},
        scratch_shapes=buffers + done,
        **params(FLOPS[2]),
    )(offs, vert, q, late, vk, vv, out, kw, vw)
    return out


FLOPS = (10**6, 3 * 10**9, 10**6)


def solution(mesh):
    placed = (
        P(("groups", "ctx"), "head"),
        P(("groups", "ctx"), "head"),
        P(("groups", "ctx"), "head"),
        P(("groups", "head"), None),
        P(("groups", "head"), None),
    )
    return jax.shard_map(
        per_device,
        mesh=mesh,
        in_specs=placed,
        out_specs=P(("groups", "ctx"), "head"),
        check_vma=False,
    )
```

```python
import functools
import math

import jax
import jax.numpy as jnp
from jax import lax
from jax.experimental import pallas as pl
from jax.experimental.pallas import tpu as pltpu
from jax.sharding import PartitionSpec as P

BLOCK = 128
BAND = 64
CHUNK = 2
NEG = -1e30


def ring(block, axis, distance):
    size = lax.axis_size(axis)
    return lax.ppermute(block, axis, [(i, (i + distance) % size) for i in range(size)])


def line(block, axis, distance):
    size = lax.axis_size(axis)
    return lax.ppermute(block, axis, [(i, i + distance) for i in range(size - distance)])


def start_all(copies):
    for copy in copies:
        copy.start()


def wait_all(copies):
    for copy in copies:
        copy.wait()


def copies_of(pairs, sems):
    return [pltpu.make_async_copy(src, dst, sems.at[i]) for i, (src, dst) in enumerate(pairs)]


def block_at(block):
    return pl.ds(pl.multiple_of(block * BLOCK, BLOCK), BLOCK)


def listed_in(vert, shard, per_shard):
    block = jnp.int32(-1)
    for v in range(vert.shape[1]):
        local = vert[0, v] - shard * per_shard
        block = jnp.where((local >= 0) & (local < per_shard), local, block)
    return block


def early_block(vert, shard, per_shard):
    listed = listed_in(vert, shard, per_shard)
    half = per_shard // 2
    return jnp.where((listed >= 0) & (listed < half), listed, half - 1)


def late_block(early, j):
    return jnp.where(j >= early, j + 1, j)


def is_listed(half, vert):
    found = lax.shift_right_arithmetic(half, 1) == vert[0, 0]
    for v in range(1, vert.shape[1]):
        found = found | (lax.shift_right_arithmetic(half, 1) == vert[0, v])
    return found


def run_stages(bodies, after):
    order = [(0, 0)]
    for u in range(len(bodies)):
        order += [(u + 1, 0)] * (u + 1 < len(bodies)) + [(u, 1), (u, 2)]
    done = 0
    for u, _ in order:
        stores = next(bodies[u]) or []
        for ref, index, value in stores:
            ref[index] = value
        if stores:
            done += 1
            after(done)


def pick_kernel(vert_hbm, k_hbm, v_hbm, mine, early, vert, kw, vw, sems):
    tok, dim = k_hbm.shape
    own = pl.ds(tok, tok)
    loads = copies_of([(vert_hbm, vert), (k_hbm, kw.at[own, :]), (v_hbm, vw.at[own, :])], sems)
    start_all(loads)
    rank = lax.axis_index("ctx")

    @pl.when(rank == 0)
    def _():
        zero = jnp.zeros((tok, dim), jnp.bfloat16)
        kw[pl.ds(0, tok), :] = zero
        vw[pl.ds(0, tok), :] = zero

    wait_all(loads)
    per_shard = tok // BLOCK
    half = per_shard // 2
    listed = jnp.maximum(listed_in(vert, rank, per_shard), 0)
    moved = early_block(vert, rank, per_shard)
    for i, w in enumerate((kw, vw)):
        at = i * (half + 1) * BLOCK
        early[pl.ds(at, half * BLOCK), :] = w[pl.ds(tok + half * BLOCK, half * BLOCK), :]
        early[pl.ds(at + half * BLOCK, BLOCK), :] = w[block_at(per_shard + moved), :]
        mine[pl.ds(i * BLOCK, BLOCK), :] = w[block_at(per_shard + listed), :]


def load_kernel(vert, offs_hbm, q_hbm, kw, vw, late, offs, q_ref, sems):
    loads = copies_of([(offs_hbm, offs), (q_hbm, q_ref)], sems)
    start_all(loads)
    per_shard = kw.shape[0] // BLOCK // 2
    half = per_shard // 2
    moved = early_block(vert, lax.axis_index("ctx"), per_shard)
    for i, w in enumerate((kw, vw)):
        for j in range(half - 1):
            late[pl.ds((i * (half - 1) + j) * BLOCK, BLOCK), :] = w[block_at(per_shard + late_block(moved, j)), :]
    wait_all(loads)


def attend_rows(groups, unroll, base, o_hbm, offs, vert, q_ref, kw, vw, vk, vv, o_buf, o_sems, heads, dim):
    tok = q_ref.shape[0]
    rows = heads * BAND
    listed = vert.shape[1]
    first = lax.axis_index("ctx") * (tok // BAND)
    scale = dim**-0.5 * math.log2(math.e)
    group = unroll * BAND
    r_at = lax.broadcasted_iota(jnp.int32, (BAND, BLOCK), 0)
    t_at = lax.broadcasted_iota(jnp.int32, (BAND, BLOCK), 1)
    mask = jnp.where((t_at > r_at) & (t_at <= r_at + BAND), 0.0, NEG)

    def row_block(a):
        keys, values, biases = [], [], []
        for s in range(offs.shape[1]):
            low = a - lax.div(offs[0, s], BAND) - 1
            at = pl.ds(pl.multiple_of(tok + low * BAND, BAND), BLOCK)
            keys.append(kw[at, :])
            values.append(vw[at, :])
            hidden = [(first + h < 0) | is_listed(first + h, vert) for h in (low, low + 1)]
            column = [jnp.where(h, jnp.float32(NEG), jnp.float32(0)) for h in hidden]
            biases.append(mask + jnp.where(t_at < BAND, column[0], column[1]))
        for v in range(listed):
            reach = (first + a) * BAND - vert[0, v] * BLOCK
            biases.append(jnp.where(t_at - r_at <= reach, 0.0, NEG))
        at = pl.ds(pl.multiple_of(a * BAND, BAND), BAND)
        q = jnp.concatenate([q_ref[at, h * dim : (h + 1) * dim] for h in range(heads)], 0)
        keys = jnp.concatenate(keys + [vk[...]], 0)
        scores = lax.dot_general(q, keys, (((1,), (1,)), ((), ())), preferred_element_type=jnp.float32)
        parts = [
            (scores[:, i * BLOCK : (i + 1) * BLOCK].reshape(heads, BAND, BLOCK) + bias[None]).reshape(rows, BLOCK)
            for i, bias in enumerate(biases)
        ]
        yield
        top = jnp.max(functools.reduce(jnp.maximum, parts), axis=-1, keepdims=True)
        rounded = jnp.concatenate([jnp.exp2((x - top) * scale).astype(jnp.bfloat16) for x in parts], 1)
        yield
        values = jnp.concatenate(values + [vv[...]], 0)
        values = jnp.concatenate([values, jnp.ones_like(values)], 1)
        acc = jnp.dot(rounded, values, preferred_element_type=jnp.float32)
        out = (acc[:, :dim] / acc[:, dim:]).astype(jnp.bfloat16)
        yield [(o_buf, (at, slice(h * dim, (h + 1) * dim)), out[h * BAND : (h + 1) * BAND]) for h in range(heads)]

    chunk = min(unroll, CHUNK)

    def out_copy(c):
        at = pl.ds(pl.multiple_of((base + c * chunk) * BAND, chunk * BAND), chunk * BAND)
        return pltpu.make_async_copy(o_buf.at[at, :], o_hbm.at[at, :], o_sems.at[c])

    def step(g, carry):
        def after(done):
            if done % chunk == 0:
                out_copy(g * (unroll // chunk) + done // chunk - 1).start()

        run_stages([row_block(base + g * unroll + u) for u in range(unroll)], after)
        return carry

    lax.fori_loop(0, groups, step, 0)
    for c in range(groups * unroll // chunk):
        out_copy(c).wait()


def load_listed(vert, rank, k_own, v_own, vk, vv, others):
    per_shard = k_own.shape[0] // BLOCK
    for v in range(vert.shape[1]):
        owner = lax.div(vert[0, v], per_shard)
        local = vert[0, v] - owner * per_shard
        dst = pl.ds(v * BLOCK, BLOCK)
        for here, k_src, v_src, k_block, v_block in [
            (rank <= owner, k_own, v_own, local, local),
            *others(owner, local),
        ]:

            @pl.when(here)
            def _():
                vk[dst, :] = k_src[block_at(k_block), :]
                vv[dst, :] = v_src[block_at(v_block), :]


def first_kernel(offs, vert, q_ref, k_win, v_win, o_hbm, vk, vv, o_buf, o_sems, *, heads, dim, unroll):
    tok = q_ref.shape[0]
    own = pl.ds(tok, tok)
    rank = lax.axis_index("ctx")

    @pl.when(rank == 0)
    def _():
        load_listed(vert, rank, k_win.at[own, :], v_win.at[own, :], vk, vv, lambda owner, local: [])
        attend_rows(
            tok // BAND // unroll, unroll, 0, o_hbm, offs, vert, q_ref, k_win, v_win, vk, vv, o_buf, o_sems, heads, dim
        )


def upper_kernel(offs, vert, q_ref, early, *refs, heads, dim, direct, unroll):
    remote, (o_hbm, kw, vw, vk, vv, o_buf, o_sems) = refs[:-10][::-1], refs[-7:]
    tok = q_ref.shape[0]
    per_shard = tok // BLOCK
    half = per_shard // 2
    rank = lax.axis_index("ctx")

    @pl.when(rank > 0)
    def _():
        moved = early_block(vert, rank - 1, per_shard)
        for i, w in enumerate((kw, vw)):
            at = i * (half + 1) * BLOCK
            w[pl.ds(half * BLOCK, half * BLOCK), :] = early[pl.ds(at, half * BLOCK), :]
            w[block_at(moved), :] = early[pl.ds(at + half * BLOCK, BLOCK), :]

        def others(owner, local):
            found = [(rank == owner + 1, kw, vw, local, local)]
            if direct:
                found += [(rank == owner + 2 + i, x, x, 0, 1) for i, x in enumerate(remote)]
            else:
                found.append((rank >= owner + 2, remote[0], remote[0], 2 * owner, 2 * owner + 1))
            return found

        own = pl.ds(tok, tok)
        load_listed(vert, rank, kw.at[own, :], vw.at[own, :], vk, vv, others)
        n = tok // BAND // 2
        attend_rows(n // unroll, unroll, n, o_hbm, offs, vert, q_ref, kw, vw, vk, vv, o_buf, o_sems, heads, dim)


def lower_kernel(offs, vert, q_ref, late, vk, vv, _o, _kw, _vw, o_hbm, kw, vw, o_buf, o_sems, *, heads, dim, unroll):
    tok = q_ref.shape[0]
    per_shard = tok // BLOCK
    half = per_shard // 2
    rank = lax.axis_index("ctx")

    @pl.when(rank > 0)
    def _():
        moved = early_block(vert, rank - 1, per_shard)
        for i, w in enumerate((kw, vw)):
            for j in range(half - 1):
                w[block_at(late_block(moved, j)), :] = late[pl.ds((i * (half - 1) + j) * BLOCK, BLOCK), :]
        n = tok // BAND // 2
        attend_rows(n // unroll, unroll, 0, o_hbm, offs, vert, q_ref, kw, vw, vk, vv, o_buf, o_sems, heads, dim)


def per_device(queries, key_states, value_states, vertical, offsets):
    tok, dim = key_states.shape
    heads = queries.shape[1] // dim
    listed = vertical.shape[1]
    n_ctx = lax.axis_size("ctx")
    half = tok // BLOCK // 2
    bf16 = jnp.bfloat16
    hbm = pl.BlockSpec(memory_space=pl.ANY)
    pinned = [
        pltpu.with_memory_space_constraint(x, pltpu.HBM)
        for x in (offsets, vertical, queries, key_states, value_states)
    ]
    vmem, smem = pl.BlockSpec(memory_space=pltpu.VMEM), pl.BlockSpec(memory_space=pltpu.SMEM)

    def params(flops, limit=24):
        return dict(
            compiler_params=pltpu.CompilerParams(vmem_limit_bytes=limit * 2**20),
            cost_estimate=pl.CostEstimate(flops=flops, bytes_accessed=2**20, transcendentals=0),
        )

    window, blocks = (2 * tok, dim), (listed * BLOCK, dim)
    mine, early, vert, kw, vw = pl.pallas_call(
        pick_kernel,
        out_shape=[pltpu.VMEM((2 * n * BLOCK, dim), bf16) for n in (1, half + 1)]
        + [pltpu.SMEM(vertical.shape, jnp.int32)]
        + [pltpu.VMEM(window, bf16)] * 2,
        in_specs=[hbm] * 3,
        out_specs=[vmem, vmem, smem, vmem, vmem],
        scratch_shapes=[pltpu.SemaphoreType.DMA((3,))],
        **params(10**6),
    )(pinned[1], pinned[3], pinned[4])
    early = ring(early, "ctx", 1)
    direct = n_ctx <= 4
    if direct:
        remote = [line(mine, "ctx", d) for d in range(2, n_ctx)]
    else:
        remote = [lax.all_gather(mine, "ctx", axis=0, tiled=True)]
    late, offs, q = pl.pallas_call(
        load_kernel,
        out_shape=[
            pltpu.VMEM((2 * (half - 1) * BLOCK, dim), bf16),
            pltpu.SMEM(offsets.shape, jnp.int32),
            pltpu.VMEM(queries.shape, bf16),
        ],
        in_specs=[smem, hbm, hbm, vmem, vmem],
        out_specs=[vmem, smem, vmem],
        scratch_shapes=[pltpu.SemaphoreType.DMA((2,))],
        **params(10**6),
    )(vert, pinned[0], pinned[2], kw, vw)
    late = ring(late, "ctx", 1)
    unroll = (4, 8, 8) if listed <= 4 else (1, 1, 1)
    o_shape = jax.ShapeDtypeStruct(queries.shape, bf16)
    buffers = [pltpu.VMEM(queries.shape, bf16)]
    done = [pltpu.SemaphoreType.DMA((tok // BAND,))]
    out = pl.pallas_call(
        functools.partial(first_kernel, heads=heads, dim=dim, unroll=unroll[0]),
        out_shape=o_shape,
        in_specs=[smem, smem] + [vmem] * 3,
        out_specs=hbm,
        scratch_shapes=[pltpu.VMEM(blocks, bf16)] * 2 + buffers + done,
        **params(FLOPS[0]),
    )(offs, vert, q, kw, vw)
    n = 4 + len(remote)
    out, kw, vw, vk, vv = pl.pallas_call(
        functools.partial(upper_kernel, heads=heads, dim=dim, direct=direct, unroll=unroll[1]),
        out_shape=[o_shape] + [pltpu.VMEM(x, bf16) for x in (window, window, blocks, blocks)],
        in_specs=[smem, smem, vmem, vmem] + [vmem] * len(remote) + [hbm, vmem, vmem],
        out_specs=[hbm] + [vmem] * 4,
        input_output_aliases={n: 0, n + 1: 1, n + 2: 2},
        scratch_shapes=buffers + done,
        **params(FLOPS[1]),
    )(offs, vert, q, early, *remote[::-1], out, kw, vw)
    out, _, _ = pl.pallas_call(
        functools.partial(lower_kernel, heads=heads, dim=dim, unroll=unroll[2]),
        out_shape=[o_shape] + [pltpu.VMEM(window, bf16)] * 2,
        in_specs=[smem, smem] + [vmem] * 4 + [hbm, vmem, vmem],
        out_specs=[hbm] + [vmem] * 2,
        input_output_aliases={6: 0, 7: 1, 8: 2},
        scratch_shapes=buffers + done,
        **params(FLOPS[2]),
    )(offs, vert, q, late, vk, vv, out, kw, vw)
    return out


FLOPS = (10**6, 3 * 10**9, 10**6)


def solution(mesh):
    placed = (
        P(("groups", "ctx"), "head"),
        P(("groups", "ctx"), "head"),
        P(("groups", "ctx"), "head"),
        P(("groups", "head"), None),
        P(("groups", "head"), None),
    )
    return jax.shard_map(
        per_device,
        mesh=mesh,
        in_specs=placed,
        out_specs=P(("groups", "ctx"), "head"),
        check_vma=False,
    )
```

```python
import functools
import math

import jax
import jax.numpy as jnp
from jax import lax
from jax.experimental import pallas as pl
from jax.experimental.pallas import tpu as pltpu
from jax.sharding import PartitionSpec as P

BLOCK = 128
BAND = 64
CHUNK = 2
NEG = -1e30


def ring(block, axis, distance):
    size = lax.axis_size(axis)
    return lax.ppermute(block, axis, [(i, (i + distance) % size) for i in range(size)])


def line(block, axis, distance):
    size = lax.axis_size(axis)
    return lax.ppermute(block, axis, [(i, i + distance) for i in range(size - distance)])


def start_all(copies):
    for copy in copies:
        copy.start()


def wait_all(copies):
    for copy in copies:
        copy.wait()


def copies_of(pairs, sems):
    return [pltpu.make_async_copy(src, dst, sems.at[i]) for i, (src, dst) in enumerate(pairs)]


def block_at(block):
    return pl.ds(pl.multiple_of(block * BLOCK, BLOCK), BLOCK)


def listed_in(vert, shard, per_shard):
    block = jnp.int32(-1)
    for v in range(vert.shape[1]):
        local = vert[0, v] - shard * per_shard
        block = jnp.where((local >= 0) & (local < per_shard), local, block)
    return block


def early_block(vert, shard, per_shard):
    listed = listed_in(vert, shard, per_shard)
    half = per_shard // 2
    return jnp.where((listed >= 0) & (listed < half), listed, half - 1)


def late_block(early, j):
    return jnp.where(j >= early, j + 1, j)


def is_listed(half, vert):
    found = lax.shift_right_arithmetic(half, 1) == vert[0, 0]
    for v in range(1, vert.shape[1]):
        found = found | (lax.shift_right_arithmetic(half, 1) == vert[0, v])
    return found


def run_stages(bodies, after):
    order = [(0, 0)]
    for u in range(len(bodies)):
        order += [(u + 1, 0)] * (u + 1 < len(bodies)) + [(u, 1), (u, 2)]
    done = 0
    for u, _ in order:
        stores = next(bodies[u]) or []
        for ref, index, value in stores:
            ref[index] = value
        if stores:
            done += 1
            after(done)


def pick_kernel(vert_hbm, k_hbm, v_hbm, mine, early, vert, kw, vw, sems):
    tok, dim = k_hbm.shape
    own = pl.ds(tok, tok)
    loads = copies_of([(vert_hbm, vert), (k_hbm, kw.at[own, :]), (v_hbm, vw.at[own, :])], sems)
    start_all(loads)
    rank = lax.axis_index("ctx")

    @pl.when(rank == 0)
    def _():
        zero = jnp.zeros((tok, dim), jnp.bfloat16)
        kw[pl.ds(0, tok), :] = zero
        vw[pl.ds(0, tok), :] = zero

    wait_all(loads)
    per_shard = tok // BLOCK
    half = per_shard // 2
    listed = jnp.maximum(listed_in(vert, rank, per_shard), 0)
    moved = early_block(vert, rank, per_shard)
    for i, w in enumerate((kw, vw)):
        at = i * (half + 1) * BLOCK
        early[pl.ds(at, half * BLOCK), :] = w[pl.ds(tok + half * BLOCK, half * BLOCK), :]
        early[pl.ds(at + half * BLOCK, BLOCK), :] = w[block_at(per_shard + moved), :]
        mine[pl.ds(i * BLOCK, BLOCK), :] = w[block_at(per_shard + listed), :]


def load_kernel(vert, offs_hbm, q_hbm, kw, vw, late, offs, q_ref, sems):
    loads = copies_of([(offs_hbm, offs), (q_hbm, q_ref)], sems)
    start_all(loads)
    per_shard = kw.shape[0] // BLOCK // 2
    half = per_shard // 2
    moved = early_block(vert, lax.axis_index("ctx"), per_shard)
    for i, w in enumerate((kw, vw)):
        for j in range(half - 1):
            late[pl.ds((i * (half - 1) + j) * BLOCK, BLOCK), :] = w[block_at(per_shard + late_block(moved, j)), :]
    wait_all(loads)


def attend_rows(groups, unroll, base, o_hbm, offs, vert, q_ref, kw, vw, vk, vv, o_buf, o_sems, heads, dim):
    tok = q_ref.shape[0]
    listed = vert.shape[1]
    parts_of = (range(0, (heads + 1) // 2), range((heads + 1) // 2, heads))
    first = lax.axis_index("ctx") * (tok // BAND)
    scale = dim**-0.5 * math.log2(math.e)
    group = unroll * BAND
    r_at = lax.broadcasted_iota(jnp.int32, (BAND, BLOCK), 0)
    t_at = lax.broadcasted_iota(jnp.int32, (BAND, BLOCK), 1)
    mask = jnp.where((t_at > r_at) & (t_at <= r_at + BAND), 0.0, NEG)

    def row_block(a, some):
        rows = len(some) * BAND
        keys, values, biases = [], [], []
        for s in range(offs.shape[1]):
            low = a - lax.div(offs[0, s], BAND) - 1
            at = pl.ds(pl.multiple_of(tok + low * BAND, BAND), BLOCK)
            keys.append(kw[at, :])
            values.append(vw[at, :])
            hidden = [(first + h < 0) | is_listed(first + h, vert) for h in (low, low + 1)]
            column = [jnp.where(h, jnp.float32(NEG), jnp.float32(0)) for h in hidden]
            biases.append(mask + jnp.where(t_at < BAND, column[0], column[1]))
        for v in range(listed):
            reach = (first + a) * BAND - vert[0, v] * BLOCK
            biases.append(jnp.where(t_at - r_at <= reach, 0.0, NEG))
        at = pl.ds(pl.multiple_of(a * BAND, BAND), BAND)
        q = jnp.concatenate([q_ref[at, h * dim : (h + 1) * dim] for h in some], 0)
        keys = jnp.concatenate(keys + [vk[...]], 0)
        scores = lax.dot_general(q, keys, (((1,), (1,)), ((), ())), preferred_element_type=jnp.float32)
        parts = [
            (scores[:, i * BLOCK : (i + 1) * BLOCK].reshape(len(some), BAND, BLOCK) + bias[None]).reshape(rows, BLOCK)
            for i, bias in enumerate(biases)
        ]
        yield
        top = jnp.max(functools.reduce(jnp.maximum, parts), axis=-1, keepdims=True)
        rounded = jnp.concatenate([jnp.exp2((x - top) * scale).astype(jnp.bfloat16) for x in parts], 1)
        yield
        values = jnp.concatenate(values + [vv[...]], 0)
        values = jnp.concatenate([values, jnp.ones_like(values)], 1)
        acc = jnp.dot(rounded, values, preferred_element_type=jnp.float32)
        out = (acc[:, :dim] / acc[:, dim:]).astype(jnp.bfloat16)
        yield [(o_buf, (at, slice(h * dim, (h + 1) * dim)), out[i * BAND : (i + 1) * BAND]) for i, h in enumerate(some)]

    chunk = min(unroll, CHUNK)

    def out_copy(c):
        at = pl.ds(pl.multiple_of((base + c * chunk) * BAND, chunk * BAND), chunk * BAND)
        return pltpu.make_async_copy(o_buf.at[at, :], o_hbm.at[at, :], o_sems.at[c])

    def step(g, carry):
        def after(done):
            if done % (2 * chunk) == 0:
                out_copy(g * (unroll // chunk) + done // (2 * chunk) - 1).start()

        run_stages([row_block(base + g * unroll + u, some) for u in range(unroll) for some in parts_of], after)
        return carry

    lax.fori_loop(0, groups, step, 0)
    for c in range(groups * unroll // chunk):
        out_copy(c).wait()


def load_listed(vert, rank, k_own, v_own, vk, vv, others):
    per_shard = k_own.shape[0] // BLOCK
    for v in range(vert.shape[1]):
        owner = lax.div(vert[0, v], per_shard)
        local = vert[0, v] - owner * per_shard
        dst = pl.ds(v * BLOCK, BLOCK)
        for here, k_src, v_src, k_block, v_block in [
            (rank <= owner, k_own, v_own, local, local),
            *others(owner, local),
        ]:

            @pl.when(here)
            def _():
                vk[dst, :] = k_src[block_at(k_block), :]
                vv[dst, :] = v_src[block_at(v_block), :]


def first_kernel(offs, vert, q_ref, k_win, v_win, o_hbm, vk, vv, o_buf, o_sems, *, heads, dim, unroll):
    tok = q_ref.shape[0]
    own = pl.ds(tok, tok)
    rank = lax.axis_index("ctx")

    @pl.when(rank == 0)
    def _():
        load_listed(vert, rank, k_win.at[own, :], v_win.at[own, :], vk, vv, lambda owner, local: [])
        attend_rows(
            tok // BAND // unroll, unroll, 0, o_hbm, offs, vert, q_ref, k_win, v_win, vk, vv, o_buf, o_sems, heads, dim
        )


def upper_kernel(offs, vert, q_ref, early, *refs, heads, dim, direct, unroll):
    remote, (o_hbm, kw, vw, vk, vv, o_buf, o_sems) = refs[:-10][::-1], refs[-7:]
    tok = q_ref.shape[0]
    per_shard = tok // BLOCK
    half = per_shard // 2
    rank = lax.axis_index("ctx")

    @pl.when(rank > 0)
    def _():
        moved = early_block(vert, rank - 1, per_shard)
        for i, w in enumerate((kw, vw)):
            at = i * (half + 1) * BLOCK
            w[pl.ds(half * BLOCK, half * BLOCK), :] = early[pl.ds(at, half * BLOCK), :]
            w[block_at(moved), :] = early[pl.ds(at + half * BLOCK, BLOCK), :]

        def others(owner, local):
            found = [(rank == owner + 1, kw, vw, local, local)]
            if direct:
                found += [(rank == owner + 2 + i, x, x, 0, 1) for i, x in enumerate(remote)]
            else:
                found.append((rank >= owner + 2, remote[0], remote[0], 2 * owner, 2 * owner + 1))
            return found

        own = pl.ds(tok, tok)
        load_listed(vert, rank, kw.at[own, :], vw.at[own, :], vk, vv, others)
        n = tok // BAND // 2
        attend_rows(n // unroll, unroll, n, o_hbm, offs, vert, q_ref, kw, vw, vk, vv, o_buf, o_sems, heads, dim)


def lower_kernel(offs, vert, q_ref, late, vk, vv, _o, _kw, _vw, o_hbm, kw, vw, o_buf, o_sems, *, heads, dim, unroll):
    tok = q_ref.shape[0]
    per_shard = tok // BLOCK
    half = per_shard // 2
    rank = lax.axis_index("ctx")

    @pl.when(rank > 0)
    def _():
        moved = early_block(vert, rank - 1, per_shard)
        for i, w in enumerate((kw, vw)):
            for j in range(half - 1):
                w[block_at(late_block(moved, j)), :] = late[pl.ds((i * (half - 1) + j) * BLOCK, BLOCK), :]
        n = tok // BAND // 2
        attend_rows(n // unroll, unroll, 0, o_hbm, offs, vert, q_ref, kw, vw, vk, vv, o_buf, o_sems, heads, dim)


def per_device(queries, key_states, value_states, vertical, offsets):
    tok, dim = key_states.shape
    heads = queries.shape[1] // dim
    listed = vertical.shape[1]
    n_ctx = lax.axis_size("ctx")
    half = tok // BLOCK // 2
    bf16 = jnp.bfloat16
    hbm = pl.BlockSpec(memory_space=pl.ANY)
    pinned = [
        pltpu.with_memory_space_constraint(x, pltpu.HBM)
        for x in (offsets, vertical, queries, key_states, value_states)
    ]
    vmem, smem = pl.BlockSpec(memory_space=pltpu.VMEM), pl.BlockSpec(memory_space=pltpu.SMEM)

    def params(flops, limit=24):
        return dict(
            compiler_params=pltpu.CompilerParams(vmem_limit_bytes=limit * 2**20),
            cost_estimate=pl.CostEstimate(flops=flops, bytes_accessed=2**20, transcendentals=0),
        )

    window, blocks = (2 * tok, dim), (listed * BLOCK, dim)
    mine, early, vert, kw, vw = pl.pallas_call(
        pick_kernel,
        out_shape=[pltpu.VMEM((2 * n * BLOCK, dim), bf16) for n in (1, half + 1)]
        + [pltpu.SMEM(vertical.shape, jnp.int32)]
        + [pltpu.VMEM(window, bf16)] * 2,
        in_specs=[hbm] * 3,
        out_specs=[vmem, vmem, smem, vmem, vmem],
        scratch_shapes=[pltpu.SemaphoreType.DMA((3,))],
        **params(10**6),
    )(pinned[1], pinned[3], pinned[4])
    early = ring(early, "ctx", 1)
    direct = n_ctx <= 4
    if direct:
        remote = [line(mine, "ctx", d) for d in range(2, n_ctx)]
    else:
        remote = [lax.all_gather(mine, "ctx", axis=0, tiled=True)]
    late, offs, q = pl.pallas_call(
        load_kernel,
        out_shape=[
            pltpu.VMEM((2 * (half - 1) * BLOCK, dim), bf16),
            pltpu.SMEM(offsets.shape, jnp.int32),
            pltpu.VMEM(queries.shape, bf16),
        ],
        in_specs=[smem, hbm, hbm, vmem, vmem],
        out_specs=[vmem, smem, vmem],
        scratch_shapes=[pltpu.SemaphoreType.DMA((2,))],
        **params(10**6),
    )(vert, pinned[0], pinned[2], kw, vw)
    late = ring(late, "ctx", 1)
    unroll = (4, 8, 8) if listed <= 4 else (1, 1, 1)
    o_shape = jax.ShapeDtypeStruct(queries.shape, bf16)
    buffers = [pltpu.VMEM(queries.shape, bf16)]
    done = [pltpu.SemaphoreType.DMA((tok // BAND,))]
    out = pl.pallas_call(
        functools.partial(first_kernel, heads=heads, dim=dim, unroll=unroll[0]),
        out_shape=o_shape,
        in_specs=[smem, smem] + [vmem] * 3,
        out_specs=hbm,
        scratch_shapes=[pltpu.VMEM(blocks, bf16)] * 2 + buffers + done,
        **params(FLOPS[0]),
    )(offs, vert, q, kw, vw)
    n = 4 + len(remote)
    out, kw, vw, vk, vv = pl.pallas_call(
        functools.partial(upper_kernel, heads=heads, dim=dim, direct=direct, unroll=unroll[1]),
        out_shape=[o_shape] + [pltpu.VMEM(x, bf16) for x in (window, window, blocks, blocks)],
        in_specs=[smem, smem, vmem, vmem] + [vmem] * len(remote) + [hbm, vmem, vmem],
        out_specs=[hbm] + [vmem] * 4,
        input_output_aliases={n: 0, n + 1: 1, n + 2: 2},
        scratch_shapes=buffers + done,
        **params(FLOPS[1]),
    )(offs, vert, q, early, *remote[::-1], out, kw, vw)
    out, _, _ = pl.pallas_call(
        functools.partial(lower_kernel, heads=heads, dim=dim, unroll=unroll[2]),
        out_shape=[o_shape] + [pltpu.VMEM(window, bf16)] * 2,
        in_specs=[smem, smem] + [vmem] * 4 + [hbm, vmem, vmem],
        out_specs=[hbm] + [vmem] * 2,
        input_output_aliases={6: 0, 7: 1, 8: 2},
        scratch_shapes=buffers + done,
        **params(FLOPS[2]),
    )(offs, vert, q, late, vk, vv, out, kw, vw)
    return out


FLOPS = (10**6, 3 * 10**9, 10**6)


def solution(mesh):
    placed = (
        P(("groups", "ctx"), "head"),
        P(("groups", "ctx"), "head"),
        P(("groups", "ctx"), "head"),
        P(("groups", "head"), None),
        P(("groups", "head"), None),
    )
    return jax.shard_map(
        per_device,
        mesh=mesh,
        in_specs=placed,
        out_specs=P(("groups", "ctx"), "head"),
        check_vma=False,
    )
```
